32 devices in a mesh: cls: 8 (over z, core), ptl: 4 (over y, x).
Axes of the slice: x: 2, y: 2, z: 4, core: 2. Of those that a mesh axis runs over, the one named last changes fastest.
Arguments:
- images: bfloat16 [512, 256, 256], P(('cls', 'ptl')), may hold values from -6 to 6
- class_block: int32 [512, 1], P(('cls', 'ptl')), may hold values from 0 to 7; in each aligned block of 16 rows (0 to 15, 16 to 31, ...) at most 4 rows name the same one
- class_within: int32 [512], P(('cls', 'ptl')), may hold values from 0 to 24
- rotation: int32 [512], P(('cls', 'ptl')), may hold values from 0 to 3
- shift: int32 [512, 2], P(('cls', 'ptl')), may hold values from -8 to 8
- group: int32 [512], P(('cls', 'ptl')), may hold values from 0 to 63
- defocus: float32 [64], replicated, may hold values from 100 to 1000
Outputs:
- class_average: float32 [200, 2, 256, 256], P('cls', None, 'ptl')
The draws below stay inside these ranges and needn't reach their ends.
Inputs may be any that keep to these rules, and one draw needn't show every extreme that they name: `class_block`: among the particles of one device at most 4 share a class block, and in every draw some device has exactly 4 in some block.
All inputs are finite; a program needn't handle non-finite values.
Results may differ from the reference program's by a relative error of at most 0.015.
Values may be sent and summed in bfloat16 or wider, within the bound.
A program may use at most 128 MiB of HBM per device.

```python
import math
import jax
import jax.numpy as jnp
import numpy as np
from jax import lax

L = 256
CLS_DEV = 25
P_DEV = 16
GROUPS = 64
SHIFT = 8
CLASSES = 200
CAP = 4
PARTICLES = 512
N_CLS = 8
N_PTL = 4


def with_ends(values, key, smallest, largest):
    shape = values.shape
    place = [jax.random.randint(jax.random.fold_in(key, axis), (), 0, shape[axis]) for axis in range(len(shape))]
    values = values.at[tuple(place)].set(smallest)
    longest = shape.index(max(shape))
    place[longest] = (place[longest] + 1) % shape[longest]
    return values.at[tuple(place)].set(largest)


def levels(own_key, dims, pieces, smallest, largest):
    level, own = 1.0, jax.random.fold_in(own_key, 6)
    for axis_at, parts in pieces:
        draws = jnp.exp(jax.random.uniform(jax.random.fold_in(own, axis_at), (parts,), jnp.float32, smallest / len(pieces), largest / len(pieces)))
        level = level * jnp.repeat(draws, dims[axis_at] // parts).reshape([-1 if axis == axis_at else 1 for axis in range(len(dims))])
    return level


def assign_block(key, own, number, rows, count, top, bound, slope):
    order = jax.random.permutation(key, count)
    crowded, common = portions_of(count, rows * top, bound, slope, True), portions_of(count, rows * top, bound, slope, False)
    places = jnp.arange(count)

    def named(lengths, turn):
        used = int((lengths > 0).sum())
        fixed = max(1, used // 4)
        moved = fixed + (places - fixed + turn * (used - fixed)) % max(1, count - fixed)
        return jnp.zeros((count,), jnp.int32).at[order[jnp.where(places < fixed, places, moved)]].set(jnp.asarray(lengths, jnp.int32))

    lengths = jnp.where(number % 4 == 0, named(crowded, number // 4), named(common, number - number // 4 - 1))
    mixed = jax.random.permutation(jax.random.fold_in(own, 3), count)
    giver, taker = mixed[0:count // 2 * 2:2], mixed[1:count // 2 * 2:2]
    margin = jnp.minimum(lengths[giver] - 1, bound - lengths[taker]) // 2
    margin = jnp.where((giver == order[0]) | (taker == order[0]) | (lengths[taker] == 0), 0, jnp.maximum(margin, 0))
    moved = jax.random.randint(jax.random.fold_in(own, 4), (count // 2,), 0, 1 << 20) % (margin + 1)
    lengths = lengths.at[giver].add(-moved).at[taker].add(moved)
    items = jnp.searchsorted(jnp.cumsum(lengths), jnp.arange(rows * top), side="right").astype(jnp.int32)
    listing = items.reshape(top, rows).T
    listing = listing[jax.random.permutation(jax.random.fold_in(own, 1), rows)]
    turn = jax.random.randint(jax.random.fold_in(own, 2), (rows, 1), 0, top)
    return jnp.take_along_axis(listing, (jnp.arange(top)[None, :] + turn) % top, axis=1)


def portions_of(number_of, total, most, slope, full):
    portions = [(1 << 20) // math.isqrt(grade ** slope) + 1 for grade in range(1, number_of + 1)]
    largest = most if full else min(most, max(-(-total // number_of), total * portions[0] // sum(portions)))
    least = 1 if total - largest >= number_of - 1 else 0
    counts, spare = [largest] + [least] * (number_of - 1), total - largest - least * (number_of - 1)
    while spare > 0:
        free = [i for i in range(1, number_of) if counts[i] < largest] or [i for i in range(1, number_of) if counts[i] < most]
        mass, budget = sum([portions[i] for i in free]), spare
        for i in free:
            addition = min(most - counts[i], max(1, budget * portions[i] // mass), spare)
            counts[i] = counts[i] + addition
            spare = spare - addition
    return np.array(counts)


def scatter_about(rng, dims, scale, limit, shards=(), held_as=jnp.bfloat16):
    entries = scale * jax.random.normal(rng, dims, jnp.float32)
    if shards:
        entries = entries * levels(rng, dims, shards, -0.22, 0.18)
    return jnp.clip(entries, -limit, limit).astype(held_as)


def setup_inputs(seed: int = 0) -> dict:
    arg_keys = jax.random.split(jax.random.key(seed), 8)
    images = scatter_about(arg_keys[0], (PARTICLES, L, L), 1.0, 6.0, ((0, 32),))
    class_block_keys = jax.random.split(jax.random.fold_in(arg_keys[1], 1), PARTICLES // P_DEV)
    class_block_turns = jax.random.permutation(jax.random.fold_in(arg_keys[1], 3), PARTICLES // P_DEV)
    class_block = jax.vmap(lambda own, number: assign_block(jax.random.fold_in(arg_keys[1], 2), own, number, P_DEV, N_CLS, 1, CAP, 2))(class_block_keys, class_block_turns).reshape((PARTICLES, 1))
    class_within = with_ends(jax.random.randint(arg_keys[2], (PARTICLES,), 0, CLS_DEV), jax.random.fold_in(arg_keys[2], 1), 0, CLS_DEV - 1).astype(jnp.int32)
    rotation = with_ends(jax.random.randint(arg_keys[3], (PARTICLES,), 0, 4), jax.random.fold_in(arg_keys[3], 1), 0, 3).astype(jnp.int32)
    shift = with_ends(jax.random.randint(arg_keys[4], (PARTICLES, 2), 0 - SHIFT, SHIFT + 1), jax.random.fold_in(arg_keys[4], 1), 0 - SHIFT, SHIFT).astype(jnp.int32)
    group = with_ends(jax.random.randint(arg_keys[5], (PARTICLES,), 0, GROUPS), jax.random.fold_in(arg_keys[5], 1), 0, GROUPS - 1).astype(jnp.int32)
    defocus = jnp.clip(jnp.exp(jax.random.uniform(arg_keys[6], (GROUPS,), jnp.float32, math.log(100.0), math.log(1000.0))), 100.0, 1000.0)
    return dict(images=images, class_block=class_block, class_within=class_within, rotation=rotation, shift=shift, group=group, defocus=defocus)


PHASE_CONTRAST = math.sqrt(0.99)
AMPLITUDE_CONTRAST = 0.1
WIENER_TERM = 1.0

def fourier_tables(extent):
    positions = jnp.arange(extent, dtype=jnp.int32)
    products = positions[:, None] * positions[None, :] % extent
    angles = products.astype(jnp.float32) * (2.0 * math.pi / extent)
    scale = 1.0 / math.sqrt(extent)
    cosines = (jnp.cos(angles) * scale).astype(jnp.bfloat16)
    sines = (jnp.sin(angles) * scale).astype(jnp.bfloat16)
    table_one = jnp.concatenate([cosines, sines], axis=1)
    upper = jnp.stack([cosines, -sines], axis=1)
    lower = jnp.stack([-sines, -cosines], axis=1)
    table_two = jnp.stack([upper, lower], axis=0)
    return (table_one, table_two)

def transfer(groups_of, defocus, extent):
    positions = jnp.arange(extent, dtype=jnp.int32)
    signed = jnp.where(positions < extent // 2, positions, positions - extent)
    frequency = signed.astype(jnp.float32) / extent
    radius = frequency[:, None] * frequency[:, None] + frequency[None, :] * frequency[None, :]
    matches = groups_of[:, None] == jnp.arange(defocus.shape[0], dtype=jnp.int32)[None, :]
    chosen = lax.optimization_barrier(jnp.sum(jnp.where(matches, defocus[None, :], jnp.zeros_like(defocus)[None, :]), axis=1))
    aberration = chosen[:, None, None] * radius[None]
    return -(PHASE_CONTRAST * jnp.sin(aberration) + AMPLITUDE_CONTRAST * jnp.cos(aberration))

def weighted_spectrum(pictures, labels, defocus):
    extent = pictures.shape[-1]
    quarter_turns = labels[:, 1]
    rotated = pictures
    for quarter in range(1, 4):
        rotated = jnp.where((quarter_turns == quarter)[:, None, None], jnp.rot90(pictures, quarter, axes=(1, 2)), rotated)
    table_one, table_two = fourier_tables(extent)
    halfway = jnp.einsum('syx,xk->syk', rotated.astype(jnp.float32), table_one.astype(jnp.float32))
    halfway = halfway.astype(jnp.bfloat16).reshape(pictures.shape[0], extent, 2, extent)
    spectrum = jnp.einsum('akby,sybx->sakx', table_two.astype(jnp.float32), halfway.astype(jnp.float32))
    positions = jnp.arange(extent, dtype=jnp.int32)
    phase_steps = (positions[None, :, None] * labels[:, 3][:, None, None] + positions[None, None, :] * labels[:, 2][:, None, None]) % extent
    angles = phase_steps.astype(jnp.float32) * (2.0 * math.pi / extent)
    cos_part = jnp.cos(angles)
    sine_part = jnp.sin(angles)
    real_part = spectrum[:, 0] * cos_part + spectrum[:, 1] * sine_part
    imag_part = spectrum[:, 1] * cos_part - spectrum[:, 0] * sine_part
    contrast = transfer(labels[:, 4], defocus, extent)
    weighted = jnp.stack([contrast * real_part, contrast * imag_part], axis=1).astype(jnp.bfloat16)
    squared = (contrast * contrast).astype(jnp.bfloat16)
    return (weighted, squared)

def reference(images, class_block, class_within, rotation, shift, group, defocus):
    zeros_col = jnp.zeros_like(class_within)
    ones_col = jnp.ones_like(class_within)
    labels = jnp.stack([class_within, rotation, shift[:, 0], shift[:, 1], group, ones_col, zeros_col, zeros_col], axis=1)
    klass = class_block[:, 0] * CLS_DEV + class_within
    shaped_images = images.reshape(N_CLS, N_PTL, P_DEV, L, L)
    shaped_labels = labels.reshape(N_CLS, N_PTL, P_DEV, 8)
    shaped_class = klass.reshape(N_CLS, N_PTL, P_DEV)

    def column(running, column_index):
        numer_sum, weight_sum = running
        pictures = lax.dynamic_index_in_dim(shaped_images, column_index, 1, keepdims=False).reshape(N_CLS * P_DEV, L, L)
        info = lax.dynamic_index_in_dim(shaped_labels, column_index, 1, keepdims=False).reshape(N_CLS * P_DEV, 8)
        class_ids = lax.dynamic_index_in_dim(shaped_class, column_index, 1, keepdims=False).reshape(N_CLS * P_DEV)
        weighted, squared = weighted_spectrum(pictures, info, defocus)
        numerator = jax.ops.segment_sum(weighted.astype(jnp.float32), class_ids, num_segments=CLASSES)
        weight = jax.ops.segment_sum(squared.astype(jnp.float32), class_ids, num_segments=CLASSES)
        numerator = lax.optimization_barrier(numerator.astype(jnp.bfloat16))
        return ((numer_sum + numerator.astype(jnp.float32), weight_sum + weight), None)
    start = (jnp.zeros((CLASSES, 2, L, L), jnp.float32), jnp.zeros((CLASSES, L, L), jnp.float32))
    (numerator, weight), unused = lax.scan(column, start, jnp.arange(N_PTL, dtype=jnp.int32))
    return numerator / (weight[:, None] + WIENER_TERM)
```

```python
import functools
import math

import jax
import jax.numpy as jnp
import ml_dtypes
import numpy as np
from jax import lax
from jax.experimental import pallas as pl
from jax.experimental.pallas import tpu as pltpu
from jax.sharding import PartitionSpec as P

CLS_DEV = 25
SHIFT = 8
PHASE_CONTRAST = math.sqrt(0.99)
AMPLITUDE_CONTRAST = 0.1
WIENER_TERM = 1.0
OFFSET_TURNS = math.atan2(AMPLITUDE_CONTRAST, PHASE_CONTRAST) / (2.0 * math.pi)
VMEM = 48 * 1024 * 1024


def sine_coefficients():
    t = np.cos(np.linspace(0.0, math.pi / 2, 2001)[:-1]) / 2
    basis = np.stack([t ** (2 * i + 1) for i in range(8)], axis=1)
    return [float(c) for c in np.linalg.lstsq(basis, np.sin(2 * np.pi * t), rcond=None)[0]]


SINE = sine_coefficients()


def sine_of_turns(turns):
    t = turns - jnp.round(turns)
    square = t * t
    value = jnp.full_like(t, SINE[-1])
    for coefficient in SINE[-2::-1]:
        value = value * square + coefficient
    return value * t


def packed(extent):
    half = extent // 2
    index = np.arange(extent)
    is_sine = index > half
    return np.where(is_sine, index - half, index), is_sine


def tables(extent):
    frequency, is_sine = packed(extent)
    moves = np.arange(-SHIFT, SHIFT + 2)
    angle = frequency[None, :, None] * (np.arange(extent)[None, None, :] + moves[:, None, None])
    angle = (angle % extent) * (2.0 * math.pi / extent)
    value = np.where(is_sine[None, :, None], np.sin(angle), np.cos(angle)) / math.sqrt(extent)
    rows = value.astype(ml_dtypes.bfloat16)
    return rows, np.ascontiguousarray(rows.transpose(0, 2, 1))


def row_expansion(extent, parts):
    half = extent // 2
    each = extent // parts
    out = np.zeros((parts, 2, each, extent), np.float32)
    for ky in range(extent):
        size = min(ky, extent - ky)
        out[ky // each, 0, ky % each, size] = 1.0
        if 0 < size < half:
            out[ky // each, 1, ky % each, half + size] = 1.0 if ky < half else -1.0
    return out.reshape(2 * extent, extent).astype(ml_dtypes.bfloat16)


def column_expansion(extent):
    half = extent // 2
    out = np.zeros((extent, 2, extent), np.float32)
    for kx in range(extent):
        size = min(kx, extent - kx)
        out[size, 0, kx] = 1.0
        if 0 < size < half:
            out[half + size, 1, kx] = -1.0 if kx < half else 1.0
    return out.reshape(extent, 2 * extent).astype(ml_dtypes.bfloat16)


def transform_kernel(slot, info, defocus, image, rows, columns, radius, out, turned):
    particle = pl.program_id(0)
    extent = image.shape[-1]
    turn = info[particle, 0]
    shift_x = info[particle, 1]
    shift_y = info[particle, 2]
    flip_x = turn >= 2
    flip_y = (turn == 1) | (turn == 2)
    move_x = jnp.where(flip_x, 1 - shift_x, shift_x) + SHIFT
    move_y = jnp.where(flip_y, 1 - shift_y, shift_y) + SHIFT
    odd = turn % 2 == 1

    @pl.when(odd)
    def _():
        turned[...] = image[0].T

    @pl.when(jnp.logical_not(odd))
    def _():
        turned[...] = image[0]

    along_x = jnp.dot(turned[...], columns[move_x], preferred_element_type=jnp.float32)
    spectrum = jnp.dot(
        rows[move_y], along_x.astype(jnp.bfloat16), preferred_element_type=jnp.float32
    )
    scale = defocus[info[particle, 3]] * (1.0 / (2.0 * math.pi))
    contrast = -sine_of_turns(radius[...] * scale + OFFSET_TURNS)
    half = extent // 2
    row_sine = lax.broadcasted_iota(jnp.int32, (extent, 1), 0) > half
    column_sine = lax.broadcasted_iota(jnp.int32, (1, extent), 1) > half
    sign_y = jnp.where(flip_y, -1.0, 1.0)
    sign_x = jnp.where(flip_x, -1.0, 1.0)
    signs = jnp.where(row_sine, sign_y, 1.0) * jnp.where(column_sine, sign_x, 1.0)
    out[0] = (spectrum * (contrast * signs)).astype(jnp.bfloat16)


def class_kernel(sources, capacity, number, per_step, labels, block, slots, expand, out, total):
    step = pl.program_id(0)
    loads = sources

    @pl.when(step == 0)
    def _():
        total[...] = jnp.zeros_like(total)

    @pl.when(step < loads)
    def _():
        def body(particle, filled):
            label = labels[step * number + particle]
            mine = label // CLS_DEV == block[0]

            @pl.when(mine)
            def _():
                within = label % CLS_DEV
                total[within] += slots[filled].astype(jnp.float32)

            return filled + mine.astype(jnp.int32)

        lax.fori_loop(0, number, body, jnp.int32(0))

    @pl.when(step >= loads)
    def _():
        parts, _, double, extent = out.shape
        for item in range(per_step):
            value = total[(step - loads) * per_step + item].astype(jnp.bfloat16)
            laid = jnp.dot(expand[...], value, preferred_element_type=jnp.float32)
            laid = laid.astype(jnp.bfloat16)
            for part in range(parts):
                out[part, item] = laid[part * double : (part + 1) * double]


def weight_kernel(labels, groups, block, defocus, radius, out):
    out[...] = jnp.zeros_like(out)

    def body(particle, carry):
        label = labels[particle]

        @pl.when(label // CLS_DEV == block[0])
        def _():
            scale = defocus[groups[particle]] * (1.0 / (2.0 * math.pi))
            contrast = sine_of_turns(radius[...] * scale + OFFSET_TURNS)
            within = label % CLS_DEV
            out[within] += contrast * contrast

        return carry

    lax.fori_loop(0, labels.shape[0], body, 0)


def final_kernel(per_step, received, weight, expand, out):
    parts = received.shape[0]
    _, _, each, extent = out.shape
    for item in range(per_step):
        value = received[0, item].astype(jnp.float32)
        for part in range(1, parts):
            value = value + received[part, item].astype(jnp.float32)
        wide = jnp.dot(value.astype(jnp.bfloat16), expand[...], preferred_element_type=jnp.float32)
        inverse = 1.0 / (weight[item] + WIENER_TERM)
        out[item, 0] = (wide[:each, :extent] + wide[each:, extent:]) * inverse
        out[item, 1] = (wide[:each, extent:] - wide[each:, :extent]) * inverse


def params():
    return pltpu.CompilerParams(vmem_limit_bytes=VMEM)


def per_device(images, class_block, class_within, rotation, shift, group, defocus):
    blocks = lax.axis_size("cls")
    parts = lax.axis_size("ptl")
    number, extent, _ = images.shape
    each = extent // parts
    capacity = 2 * number // blocks
    me = lax.axis_index("cls").astype(jnp.int32)
    part = lax.axis_index("ptl").astype(jnp.int32)
    target = class_block[:, 0]
    same = target[:, None] == target[None, :]
    before = jnp.arange(number)[:, None] > jnp.arange(number)[None, :]
    slot = target * capacity + jnp.sum((same & before).astype(jnp.int32), axis=1)
    info = jnp.stack([rotation, shift[:, 0], shift[:, 1], group], axis=1)

    klass = target * CLS_DEV + class_within
    own = jnp.stack([klass, group], axis=0)
    labels = lax.all_gather(own, ("cls", "ptl"), axis=0)
    labels = labels.reshape(blocks, parts, 2, number)
    all_class = labels[:, :, 0].reshape(-1)
    all_group = labels[:, :, 1].reshape(-1)
    column_class = lax.dynamic_index_in_dim(labels[:, :, 0], part, 1, keepdims=False).reshape(-1)

    frequency, _ = packed(extent)
    share = (frequency / extent) ** 2
    packed_radius = (share[:, None] + share[None, :]).astype(np.float32)
    row_table, column_table = tables(extent)

    whole = lambda shape: pl.BlockSpec(shape, lambda *_: (0,) * len(shape))
    outgoing = pl.pallas_call(
        transform_kernel,
        grid_spec=pltpu.PrefetchScalarGridSpec(
            num_scalar_prefetch=3,
            grid=(number,),
            in_specs=[
                pl.BlockSpec((1, extent, extent), lambda i, *_: (i, 0, 0)),
                whole(row_table.shape),
                whole(column_table.shape),
                whole((extent, extent)),
            ],
            out_specs=pl.BlockSpec((1, extent, extent), lambda i, slot, *_: (slot[i], 0, 0)),
            scratch_shapes=[pltpu.VMEM((extent, extent), jnp.bfloat16)],
        ),
        out_shape=jax.ShapeDtypeStruct((blocks * capacity, extent, extent), jnp.bfloat16),
        compiler_params=params(),
        name="transform",
    )(slot, info, defocus, images, row_table, column_table, packed_radius)
    arrived = lax.all_to_all(
        outgoing.reshape(blocks, capacity, extent, extent), "cls", 0, 0, tiled=True
    ).reshape(blocks * capacity, extent, extent)

    ky = part * each + jnp.arange(each, dtype=jnp.int32)
    kx = np.minimum(np.arange(extent), extent - np.arange(extent))
    ky = jnp.minimum(ky, extent - ky).astype(jnp.float32) / extent
    radius = ky[:, None] * ky[:, None] + ((kx / extent) ** 2).astype(np.float32)[None, :]
    smem = pl.BlockSpec(memory_space=pltpu.SMEM)
    vmem = pl.BlockSpec(memory_space=pltpu.VMEM)
    weight = pl.pallas_call(
        weight_kernel,
        in_specs=[smem, smem, smem, smem, vmem],
        out_specs=vmem,
        out_shape=jax.ShapeDtypeStruct((CLS_DEV, each, extent), jnp.float32),
        compiler_params=params(),
        cost_estimate=pl.CostEstimate(
            flops=40 * number * parts * each * extent, bytes_accessed=2**21, transcendentals=0
        ),
        name="weights",
    )(all_class, all_group, me[None], defocus, radius)

    per_step = 5
    steps = CLS_DEV // per_step
    partial = pl.pallas_call(
        functools.partial(class_kernel, blocks, capacity, number, per_step),
        grid_spec=pltpu.PrefetchScalarGridSpec(
            num_scalar_prefetch=2,
            grid=(blocks + steps,),
            in_specs=[
                pl.BlockSpec(
                    (capacity, extent, extent), lambda i, *_: (jnp.minimum(i, blocks - 1), 0, 0)
                ),
                whole((2 * extent, extent)),
            ],
            out_specs=pl.BlockSpec(
                (parts, per_step, 2 * each, extent),
                lambda i, *_: (0, jnp.maximum(i - blocks, 0), 0, 0),
            ),
            scratch_shapes=[pltpu.VMEM((CLS_DEV, extent, extent), jnp.float32)],
        ),
        out_shape=jax.ShapeDtypeStruct((parts, CLS_DEV, 2 * each, extent), jnp.bfloat16),
        compiler_params=params(),
        name="classes",
    )(column_class, me[None], arrived, row_expansion(extent, parts))
    received = lax.all_to_all(partial, "ptl", 0, 0, tiled=True)

    return pl.pallas_call(
        functools.partial(final_kernel, per_step),
        grid=(steps,),
        in_specs=[
            pl.BlockSpec((parts, per_step, 2 * each, extent), lambda i: (0, i, 0, 0)),
            pl.BlockSpec((per_step, each, extent), lambda i: (i, 0, 0)),
            whole((extent, 2 * extent)),
        ],
        out_specs=pl.BlockSpec((per_step, 2, each, extent), lambda i: (i, 0, 0, 0)),
        out_shape=jax.ShapeDtypeStruct((CLS_DEV, 2, each, extent), jnp.float32),
        compiler_params=params(),
        name="finish",
    )(received, weight, column_expansion(extent))


def solution(mesh):
    return jax.shard_map(
        per_device,
        mesh=mesh,
        in_specs=(
            P(("cls", "ptl"), None, None),
            P(("cls", "ptl"), None),
            P(("cls", "ptl")),
            P(("cls", "ptl")),
            P(("cls", "ptl"), None),
            P(("cls", "ptl")),
            P(),
        ),
        out_specs=P("cls", None, "ptl", None),
        check_vma=False,
    )
```

```python
import functools
import math

import jax
import jax.numpy as jnp
import ml_dtypes
import numpy as np
from jax import lax
from jax.experimental import pallas as pl
from jax.experimental.pallas import tpu as pltpu
from jax.sharding import PartitionSpec as P

CLS_DEV = 25
SHIFT = 8
PHASE_CONTRAST = math.sqrt(0.99)
AMPLITUDE_CONTRAST = 0.1
WIENER_TERM = 1.0
OFFSET_TURNS = math.atan2(AMPLITUDE_CONTRAST, PHASE_CONTRAST) / (2.0 * math.pi)
VMEM = 48 * 1024 * 1024


def sine_coefficients():
    t = np.cos(np.linspace(0.0, math.pi / 2, 2001)[:-1]) / 2
    basis = np.stack([t ** (2 * i + 1) for i in range(7)], axis=1)
    return [float(c) for c in np.linalg.lstsq(basis, np.sin(2 * np.pi * t), rcond=None)[0]]


SINE = sine_coefficients()


def sine_of_turns(turns):
    t = turns - jnp.round(turns)
    square = t * t
    value = jnp.full_like(t, SINE[-1])
    for coefficient in SINE[-2::-1]:
        value = value * square + coefficient
    return value * t


def packed(extent):
    half = extent // 2
    index = np.arange(extent)
    is_sine = index > half
    return np.where(is_sine, index - half, index), is_sine


def tables(extent):
    frequency, is_sine = packed(extent)
    moves = np.arange(-SHIFT, SHIFT + 2)
    angle = frequency[None, :, None] * (np.arange(extent)[None, None, :] + moves[:, None, None])
    angle = (angle % extent) * (2.0 * math.pi / extent)
    value = np.where(is_sine[None, :, None], np.sin(angle), np.cos(angle)) / math.sqrt(extent)
    rows = value.astype(ml_dtypes.bfloat16)
    return rows, np.ascontiguousarray(rows.transpose(0, 2, 1))


def row_expansion(extent, parts):
    half = extent // 2
    each = extent // parts
    out = np.zeros((parts, 2, each, extent), np.float32)
    for ky in range(extent):
        size = min(ky, extent - ky)
        out[ky // each, 0, ky % each, size] = 1.0
        if 0 < size < half:
            out[ky // each, 1, ky % each, half + size] = 1.0 if ky < half else -1.0
    return out.reshape(2 * extent, extent).astype(ml_dtypes.bfloat16)


def column_expansion(extent):
    half = extent // 2
    out = np.zeros((extent, 2, extent), np.float32)
    for kx in range(extent):
        size = min(kx, extent - kx)
        out[size, 0, kx] = 1.0
        if 0 < size < half:
            out[half + size, 1, kx] = -1.0 if kx < half else 1.0
    return out.reshape(extent, 2 * extent).astype(ml_dtypes.bfloat16)


def transform_kernel(slot, info, defocus, image, rows, columns, radius, out, turned):
    particle = pl.program_id(0)
    extent = image.shape[-1]
    turn = info[particle, 0]
    shift_x = info[particle, 1]
    shift_y = info[particle, 2]
    flip_x = turn >= 2
    flip_y = (turn == 1) | (turn == 2)
    move_x = jnp.where(flip_x, 1 - shift_x, shift_x) + SHIFT
    move_y = jnp.where(flip_y, 1 - shift_y, shift_y) + SHIFT
    odd = turn % 2 == 1

    @pl.when(odd)
    def _():
        turned[...] = image[0].T

    @pl.when(jnp.logical_not(odd))
    def _():
        turned[...] = image[0]

    along_x = jnp.dot(turned[...], columns[move_x], preferred_element_type=jnp.float32)
    spectrum = jnp.dot(
        rows[move_y], along_x.astype(jnp.bfloat16), preferred_element_type=jnp.float32
    )
    scale = defocus[info[particle, 3]] * (1.0 / (2.0 * math.pi))
    contrast = -sine_of_turns(radius[...] * scale + OFFSET_TURNS)
    half = extent // 2
    row_sine = lax.broadcasted_iota(jnp.int32, (extent, 1), 0) > half
    column_sine = lax.broadcasted_iota(jnp.int32, (1, extent), 1) > half
    sign_y = jnp.where(flip_y, -1.0, 1.0)
    sign_x = jnp.where(flip_x, -1.0, 1.0)
    signs = jnp.where(row_sine, sign_y, 1.0) * jnp.where(column_sine, sign_x, 1.0)
    out[0] = (spectrum * (contrast * signs)).astype(jnp.bfloat16)


def class_kernel(sources, capacity, number, per_step, labels, block, slots, expand, out, total):
    step = pl.program_id(0)
    loads = sources

    @pl.when(step == 0)
    def _():
        total[...] = jnp.zeros_like(total)

    @pl.when(step < loads)
    def _():
        def body(particle, filled):
            label = labels[step * number + particle]
            mine = label // CLS_DEV == block[0]

            @pl.when(mine)
            def _():
                within = label % CLS_DEV
                total[within] += slots[filled].astype(jnp.float32)

            return filled + mine.astype(jnp.int32)

        lax.fori_loop(0, number, body, jnp.int32(0))

    @pl.when(step >= loads)
    def _():
        parts, _, double, extent = out.shape
        for item in range(per_step):
            value = total[(step - loads) * per_step + item].astype(jnp.bfloat16)
            laid = jnp.dot(expand[...], value, preferred_element_type=jnp.float32)
            laid = laid.astype(jnp.bfloat16)
            for part in range(parts):
                out[part, item] = laid[part * double : (part + 1) * double]


def weight_kernel(labels, groups, block, defocus, radius, out):
    out[...] = jnp.zeros_like(out)

    def body(particle, carry):
        label = labels[particle]

        @pl.when(label // CLS_DEV == block[0])
        def _():
            scale = defocus[groups[particle]] * (1.0 / (2.0 * math.pi))
            contrast = sine_of_turns(radius[...] * scale + OFFSET_TURNS)
            within = label % CLS_DEV
            out[within] += contrast * contrast

        return carry

    lax.fori_loop(0, labels.shape[0], body, 0)


def final_kernel(per_step, received, weight, expand, out):
    parts = received.shape[0]
    _, _, each, extent = out.shape
    for item in range(per_step):
        value = received[0, item].astype(jnp.float32)
        for part in range(1, parts):
            value = value + received[part, item].astype(jnp.float32)
        wide = jnp.dot(value.astype(jnp.bfloat16), expand[...], preferred_element_type=jnp.float32)
        inverse = 1.0 / (weight[item] + WIENER_TERM)
        out[item, 0] = (wide[:each, :extent] + wide[each:, extent:]) * inverse
        out[item, 1] = (wide[:each, extent:] - wide[each:, :extent]) * inverse


def params():
    return pltpu.CompilerParams(vmem_limit_bytes=VMEM)


def per_device(images, class_block, class_within, rotation, shift, group, defocus):
    blocks = lax.axis_size("cls")
    parts = lax.axis_size("ptl")
    number, extent, _ = images.shape
    each = extent // parts
    capacity = 2 * number // blocks
    me = lax.axis_index("cls").astype(jnp.int32)
    part = lax.axis_index("ptl").astype(jnp.int32)
    target = class_block[:, 0]
    same = target[:, None] == target[None, :]
    before = jnp.arange(number)[:, None] > jnp.arange(number)[None, :]
    slot = target * capacity + jnp.sum((same & before).astype(jnp.int32), axis=1)
    info = jnp.stack([rotation, shift[:, 0], shift[:, 1], group], axis=1)

    klass = target * CLS_DEV + class_within
    own = jnp.stack([klass, group], axis=0)
    labels = lax.all_gather(own, ("cls", "ptl"), axis=0)
    images, labels = lax.optimization_barrier((images, labels))
    labels = labels.reshape(blocks, parts, 2, number)
    all_class = labels[:, :, 0].reshape(-1)
    all_group = labels[:, :, 1].reshape(-1)
    column_class = lax.dynamic_index_in_dim(labels[:, :, 0], part, 1, keepdims=False).reshape(-1)

    frequency, _ = packed(extent)
    share = (frequency / extent) ** 2
    packed_radius = (share[:, None] + share[None, :]).astype(np.float32)
    row_table, column_table = tables(extent)

    whole = lambda shape: pl.BlockSpec(shape, lambda *_: (0,) * len(shape))
    outgoing = pl.pallas_call(
        transform_kernel,
        grid_spec=pltpu.PrefetchScalarGridSpec(
            num_scalar_prefetch=3,
            grid=(number,),
            in_specs=[
                pl.BlockSpec((1, extent, extent), lambda i, *_: (i, 0, 0)),
                whole(row_table.shape),
                whole(column_table.shape),
                whole((extent, extent)),
            ],
            out_specs=pl.BlockSpec((1, extent, extent), lambda i, slot, *_: (slot[i], 0, 0)),
            scratch_shapes=[pltpu.VMEM((extent, extent), jnp.bfloat16)],
        ),
        out_shape=jax.ShapeDtypeStruct((blocks * capacity, extent, extent), jnp.bfloat16),
        compiler_params=params(),
        name="transform",
    )(slot, info, defocus, images, row_table, column_table, packed_radius)
    arrived = lax.all_to_all(
        outgoing.reshape(blocks, capacity, extent, extent), "cls", 0, 0, tiled=True
    ).reshape(blocks * capacity, extent, extent)

    ky = part * each + jnp.arange(each, dtype=jnp.int32)
    kx = np.minimum(np.arange(extent), extent - np.arange(extent))
    ky = jnp.minimum(ky, extent - ky).astype(jnp.float32) / extent
    radius = ky[:, None] * ky[:, None] + ((kx / extent) ** 2).astype(np.float32)[None, :]
    smem = pl.BlockSpec(memory_space=pltpu.SMEM)
    vmem = pl.BlockSpec(memory_space=pltpu.VMEM)
    weight = pl.pallas_call(
        weight_kernel,
        in_specs=[smem, smem, smem, smem, vmem],
        out_specs=vmem,
        out_shape=jax.ShapeDtypeStruct((CLS_DEV, each, extent), jnp.float32),
        compiler_params=params(),
        cost_estimate=pl.CostEstimate(
            flops=40 * number * parts * each * extent, bytes_accessed=2**21, transcendentals=0
        ),
        name="weights",
    )(all_class, all_group, me[None], defocus, radius)

    per_step = 5
    steps = CLS_DEV // per_step
    partial = pl.pallas_call(
        functools.partial(class_kernel, blocks, capacity, number, per_step),
        grid_spec=pltpu.PrefetchScalarGridSpec(
            num_scalar_prefetch=2,
            grid=(blocks + steps,),
            in_specs=[
                pl.BlockSpec(
                    (capacity, extent, extent), lambda i, *_: (jnp.minimum(i, blocks - 1), 0, 0)
                ),
                whole((2 * extent, extent)),
            ],
            out_specs=pl.BlockSpec(
                (parts, per_step, 2 * each, extent),
                lambda i, *_: (0, jnp.maximum(i - blocks, 0), 0, 0),
            ),
            scratch_shapes=[pltpu.VMEM((CLS_DEV, extent, extent), jnp.float32)],
        ),
        out_shape=jax.ShapeDtypeStruct((parts, CLS_DEV, 2 * each, extent), jnp.bfloat16),
        compiler_params=params(),
        name="classes",
    )(column_class, me[None], arrived, row_expansion(extent, parts))
    received = lax.all_to_all(partial, "ptl", 0, 0, tiled=True)

    return pl.pallas_call(
        functools.partial(final_kernel, per_step),
        grid=(steps,),
        in_specs=[
            pl.BlockSpec((parts, per_step, 2 * each, extent), lambda i: (0, i, 0, 0)),
            pl.BlockSpec((per_step, each, extent), lambda i: (i, 0, 0)),
            whole((extent, 2 * extent)),
        ],
        out_specs=pl.BlockSpec((per_step, 2, each, extent), lambda i: (i, 0, 0, 0)),
        out_shape=jax.ShapeDtypeStruct((CLS_DEV, 2, each, extent), jnp.float32),
        compiler_params=params(),
        name="finish",
    )(received, weight, column_expansion(extent))


def solution(mesh):
    return jax.shard_map(
        per_device,
        mesh=mesh,
        in_specs=(
            P(("cls", "ptl"), None, None),
            P(("cls", "ptl"), None),
            P(("cls", "ptl")),
            P(("cls", "ptl")),
            P(("cls", "ptl"), None),
            P(("cls", "ptl")),
            P(),
        ),
        out_specs=P("cls", None, "ptl", None),
        check_vma=False,
    )
```

```python
import functools
import math

import jax
import jax.numpy as jnp
import ml_dtypes
import numpy as np
from jax import lax
from jax.experimental import pallas as pl
from jax.experimental.pallas import tpu as pltpu
from jax.sharding import PartitionSpec as P

CLS_DEV = 25
SHIFT = 8
PHASE_CONTRAST = math.sqrt(0.99)
AMPLITUDE_CONTRAST = 0.1
WIENER_TERM = 1.0
OFFSET_TURNS = math.atan2(AMPLITUDE_CONTRAST, PHASE_CONTRAST) / (2.0 * math.pi)
VMEM = 48 * 1024 * 1024


def sine_coefficients():
    t = np.cos(np.linspace(0.0, math.pi / 2, 2001)[:-1]) / 2
    basis = np.stack([t ** (2 * i + 1) for i in range(7)], axis=1)
    return [float(c) for c in np.linalg.lstsq(basis, np.sin(2 * np.pi * t), rcond=None)[0]]


SINE = sine_coefficients()


def sine_of_turns(turns):
    t = turns - jnp.round(turns)
    square = t * t
    value = jnp.full_like(t, SINE[-1])
    for coefficient in SINE[-2::-1]:
        value = value * square + coefficient
    return value * t


def packed(extent):
    half = extent // 2
    index = np.arange(extent)
    is_sine = index > half
    return np.where(is_sine, index - half, index), is_sine


def tables(extent):
    frequency, is_sine = packed(extent)
    moves = np.arange(-SHIFT, SHIFT + 2)
    angle = frequency[None, :, None] * (np.arange(extent)[None, None, :] + moves[:, None, None])
    angle = (angle % extent) * (2.0 * math.pi / extent)
    value = np.where(is_sine[None, :, None], np.sin(angle), np.cos(angle)) / math.sqrt(extent)
    rows = value.astype(ml_dtypes.bfloat16)
    return rows, np.ascontiguousarray(rows.transpose(0, 2, 1))


def row_expansion(extent, parts):
    half = extent // 2
    each = extent // parts
    out = np.zeros((parts, 2, each, extent), np.float32)
    for ky in range(extent):
        size = min(ky, extent - ky)
        out[ky // each, 0, ky % each, size] = 1.0
        if 0 < size < half:
            out[ky // each, 1, ky % each, half + size] = 1.0 if ky < half else -1.0
    return out.reshape(2 * extent, extent).astype(ml_dtypes.bfloat16)


def column_expansion(extent):
    half = extent // 2
    out = np.zeros((extent, 2, extent), np.float32)
    for kx in range(extent):
        size = min(kx, extent - kx)
        out[size, 0, kx] = 1.0
        if 0 < size < half:
            out[half + size, 1, kx] = -1.0 if kx < half else 1.0
    return out.reshape(extent, 2 * extent).astype(ml_dtypes.bfloat16)


def transform_kernel(slot, info, defocus, image, rows, columns, radius, out, turned):
    particle = pl.program_id(0)
    extent = image.shape[-1]
    turn = info[particle, 0]
    shift_x = info[particle, 1]
    shift_y = info[particle, 2]
    flip_x = turn >= 2
    flip_y = (turn == 1) | (turn == 2)
    move_x = jnp.where(flip_x, 1 - shift_x, shift_x) + SHIFT
    move_y = jnp.where(flip_y, 1 - shift_y, shift_y) + SHIFT
    odd = turn % 2 == 1

    @pl.when(odd)
    def _():
        turned[...] = image[0].T

    @pl.when(jnp.logical_not(odd))
    def _():
        turned[...] = image[0]

    along_x = jnp.dot(turned[...], columns[move_x], preferred_element_type=jnp.float32)
    spectrum = jnp.dot(
        rows[move_y], along_x.astype(jnp.bfloat16), preferred_element_type=jnp.float32
    )
    scale = defocus[info[particle, 3]] * (1.0 / (2.0 * math.pi))
    contrast = -sine_of_turns(radius[...] * scale + OFFSET_TURNS)
    half = extent // 2
    row_sine = lax.broadcasted_iota(jnp.int32, (extent, 1), 0) > half
    column_sine = lax.broadcasted_iota(jnp.int32, (1, extent), 1) > half
    sign_y = jnp.where(flip_y, -1.0, 1.0)
    sign_x = jnp.where(flip_x, -1.0, 1.0)
    signs = jnp.where(row_sine, sign_y, 1.0) * jnp.where(column_sine, sign_x, 1.0)
    out[0] = (spectrum * (contrast * signs)).astype(jnp.bfloat16)


def class_kernel(sources, capacity, number, per_step, labels, block, slots, expand, out, total):
    step = pl.program_id(0)
    loads = sources

    @pl.when(step == 0)
    def _():
        total[...] = jnp.zeros_like(total)

    @pl.when(step < loads)
    def _():
        def body(particle, filled):
            label = labels[step * number + particle]
            mine = label // CLS_DEV == block[0]

            @pl.when(mine)
            def _():
                within = label % CLS_DEV
                total[within] += slots[filled].astype(jnp.float32)

            return filled + mine.astype(jnp.int32)

        lax.fori_loop(0, number, body, jnp.int32(0))

    @pl.when(step >= loads)
    def _():
        parts, _, double, extent = out.shape
        for item in range(per_step):
            value = total[(step - loads) * per_step + item].astype(jnp.bfloat16)
            laid = jnp.dot(expand[...], value, preferred_element_type=jnp.float32)
            laid = laid.astype(jnp.bfloat16)
            for part in range(parts):
                out[part, item] = laid[part * double : (part + 1) * double]


def weight_kernel(labels, groups, block, defocus, radius, out):
    out[...] = jnp.zeros_like(out)

    def body(particle, carry):
        label = labels[particle]

        @pl.when(label // CLS_DEV == block[0])
        def _():
            scale = defocus[groups[particle]] * (1.0 / (2.0 * math.pi))
            contrast = sine_of_turns(radius[...] * scale + OFFSET_TURNS)
            within = label % CLS_DEV
            out[within] += contrast * contrast

        return carry

    lax.fori_loop(0, labels.shape[0], body, 0)


def final_kernel(per_step, received, weight, expand, out):
    parts = received.shape[0]
    _, _, each, extent = out.shape
    for item in range(per_step):
        value = received[0, item].astype(jnp.float32)
        for part in range(1, parts):
            value = value + received[part, item].astype(jnp.float32)
        wide = jnp.dot(value.astype(jnp.bfloat16), expand[...], preferred_element_type=jnp.float32)
        inverse = 1.0 / (weight[item] + WIENER_TERM)
        out[item, 0] = (wide[:each, :extent] + wide[each:, extent:]) * inverse
        out[item, 1] = (wide[:each, extent:] - wide[each:, :extent]) * inverse


def params():
    return pltpu.CompilerParams(vmem_limit_bytes=VMEM)


def per_device(images, class_block, class_within, rotation, shift, group, defocus):
    blocks = lax.axis_size("cls")
    parts = lax.axis_size("ptl")
    number, extent, _ = images.shape
    each = extent // parts
    capacity = 2 * number // blocks
    me = lax.axis_index("cls").astype(jnp.int32)
    part = lax.axis_index("ptl").astype(jnp.int32)
    target = class_block[:, 0]
    same = target[:, None] == target[None, :]
    before = jnp.arange(number)[:, None] > jnp.arange(number)[None, :]
    slot = target * capacity + jnp.sum((same & before).astype(jnp.int32), axis=1)
    info = jnp.stack([rotation, shift[:, 0], shift[:, 1], group], axis=1)

    klass = target * CLS_DEV + class_within
    own = jnp.stack([klass, group], axis=0)
    column = lax.all_to_all(
        jnp.broadcast_to(own[None], (blocks, 2, number)), "cls", 0, 0, tiled=True
    )
    labels = lax.all_to_all(
        jnp.broadcast_to(column[None], (parts, blocks, 2, number)), "ptl", 0, 0, tiled=True
    )
    all_class = labels[:, :, 0].reshape(-1)
    all_group = labels[:, :, 1].reshape(-1)
    column_class = column[:, 0].reshape(-1)

    frequency, _ = packed(extent)
    share = (frequency / extent) ** 2
    packed_radius = (share[:, None] + share[None, :]).astype(np.float32)
    row_table, column_table = tables(extent)

    whole = lambda shape: pl.BlockSpec(shape, lambda *_: (0,) * len(shape))
    outgoing = pl.pallas_call(
        transform_kernel,
        grid_spec=pltpu.PrefetchScalarGridSpec(
            num_scalar_prefetch=3,
            grid=(number,),
            in_specs=[
                pl.BlockSpec((1, extent, extent), lambda i, *_: (i, 0, 0)),
                whole(row_table.shape),
                whole(column_table.shape),
                whole((extent, extent)),
            ],
            out_specs=pl.BlockSpec((1, extent, extent), lambda i, slot, *_: (slot[i], 0, 0)),
            scratch_shapes=[pltpu.VMEM((extent, extent), jnp.bfloat16)],
        ),
        out_shape=jax.ShapeDtypeStruct((blocks * capacity, extent, extent), jnp.bfloat16),
        compiler_params=params(),
        name="transform",
    )(slot, info, defocus, images, row_table, column_table, packed_radius)
    arrived = lax.all_to_all(
        outgoing.reshape(blocks, capacity, extent, extent), "cls", 0, 0, tiled=True
    ).reshape(blocks * capacity, extent, extent)

    ky = part * each + jnp.arange(each, dtype=jnp.int32)
    kx = np.minimum(np.arange(extent), extent - np.arange(extent))
    ky = jnp.minimum(ky, extent - ky).astype(jnp.float32) / extent
    radius = ky[:, None] * ky[:, None] + ((kx / extent) ** 2).astype(np.float32)[None, :]
    smem = pl.BlockSpec(memory_space=pltpu.SMEM)
    vmem = pl.BlockSpec(memory_space=pltpu.VMEM)
    weight = pl.pallas_call(
        weight_kernel,
        in_specs=[smem, smem, smem, smem, vmem],
        out_specs=vmem,
        out_shape=jax.ShapeDtypeStruct((CLS_DEV, each, extent), jnp.float32),
        compiler_params=params(),
        cost_estimate=pl.CostEstimate(
            flops=40 * number * parts * each * extent, bytes_accessed=2**21, transcendentals=0
        ),
        name="weights",
    )(all_class, all_group, me[None], defocus, radius)

    per_step = 5
    steps = CLS_DEV // per_step
    partial = pl.pallas_call(
        functools.partial(class_kernel, blocks, capacity, number, per_step),
        grid_spec=pltpu.PrefetchScalarGridSpec(
            num_scalar_prefetch=2,
            grid=(blocks + steps,),
            in_specs=[
                pl.BlockSpec(
                    (capacity, extent, extent), lambda i, *_: (jnp.minimum(i, blocks - 1), 0, 0)
                ),
                whole((2 * extent, extent)),
            ],
            out_specs=pl.BlockSpec(
                (parts, per_step, 2 * each, extent),
                lambda i, *_: (0, jnp.maximum(i - blocks, 0), 0, 0),
            ),
            scratch_shapes=[pltpu.VMEM((CLS_DEV, extent, extent), jnp.float32)],
        ),
        out_shape=jax.ShapeDtypeStruct((parts, CLS_DEV, 2 * each, extent), jnp.bfloat16),
        compiler_params=params(),
        name="classes",
    )(column_class, me[None], arrived, row_expansion(extent, parts))
    received = lax.all_to_all(partial, "ptl", 0, 0, tiled=True)

    return pl.pallas_call(
        functools.partial(final_kernel, per_step),
        grid=(steps,),
        in_specs=[
            pl.BlockSpec((parts, per_step, 2 * each, extent), lambda i: (0, i, 0, 0)),
            pl.BlockSpec((per_step, each, extent), lambda i: (i, 0, 0)),
            whole((extent, 2 * extent)),
        ],
        out_specs=pl.BlockSpec((per_step, 2, each, extent), lambda i: (i, 0, 0, 0)),
        out_shape=jax.ShapeDtypeStruct((CLS_DEV, 2, each, extent), jnp.float32),
        compiler_params=params(),
        name="finish",
    )(received, weight, column_expansion(extent))


def solution(mesh):
    return jax.shard_map(
        per_device,
        mesh=mesh,
        in_specs=(
            P(("cls", "ptl"), None, None),
            P(("cls", "ptl"), None),
            P(("cls", "ptl")),
            P(("cls", "ptl")),
            P(("cls", "ptl"), None),
            P(("cls", "ptl")),
            P(),
        ),
        out_specs=P("cls", None, "ptl", None),
        check_vma=False,
    )
```

```python
import functools
import math

import jax
import jax.numpy as jnp
import ml_dtypes
import numpy as np
from jax import lax
from jax.experimental import pallas as pl
from jax.experimental.pallas import tpu as pltpu
from jax.sharding import PartitionSpec as P

CLS_DEV = 25
SHIFT = 8
PHASE_CONTRAST = math.sqrt(0.99)
AMPLITUDE_CONTRAST = 0.1
WIENER_TERM = 1.0
OFFSET_TURNS = math.atan2(AMPLITUDE_CONTRAST, PHASE_CONTRAST) / (2.0 * math.pi)
VMEM = 48 * 1024 * 1024


def sine_coefficients():
    t = np.cos(np.linspace(0.0, math.pi / 2, 2001)[:-1]) / 2
    basis = np.stack([t ** (2 * i + 1) for i in range(7)], axis=1)
    return [float(c) for c in np.linalg.lstsq(basis, np.sin(2 * np.pi * t), rcond=None)[0]]


SINE = sine_coefficients()


def sine_of_turns(turns):
    t = turns - jnp.round(turns)
    square = t * t
    value = jnp.full_like(t, SINE[-1])
    for coefficient in SINE[-2::-1]:
        value = value * square + coefficient
    return value * t


def packed(extent):
    half = extent // 2
    index = np.arange(extent)
    is_sine = index > half
    return np.where(is_sine, index - half, index), is_sine


def tables(extent):
    frequency, is_sine = packed(extent)
    moves = np.arange(-SHIFT, SHIFT + 2)
    angle = frequency[None, :, None] * (np.arange(extent)[None, None, :] + moves[:, None, None])
    angle = (angle % extent) * (2.0 * math.pi / extent)
    value = np.where(is_sine[None, :, None], np.sin(angle), np.cos(angle)) / math.sqrt(extent)
    rows = value.astype(ml_dtypes.bfloat16)
    return rows, np.ascontiguousarray(rows.transpose(0, 2, 1))


def row_expansion(extent, parts):
    half = extent // 2
    each = extent // parts
    out = np.zeros((parts, 2, each, extent), np.float32)
    for ky in range(extent):
        size = min(ky, extent - ky)
        out[ky // each, 0, ky % each, size] = 1.0
        if 0 < size < half:
            out[ky // each, 1, ky % each, half + size] = 1.0 if ky < half else -1.0
    return out.reshape(2 * extent, extent).astype(ml_dtypes.bfloat16)


def column_expansion(extent):
    half = extent // 2
    out = np.zeros((extent, 2, extent), np.float32)
    for kx in range(extent):
        size = min(kx, extent - kx)
        out[size, 0, kx] = 1.0
        if 0 < size < half:
            out[half + size, 1, kx] = -1.0 if kx < half else 1.0
    return out.reshape(extent, 2 * extent).astype(ml_dtypes.bfloat16)


def transform_kernel(slot, info, defocus, image, rows, columns, radius, low, high, turned):
    particle = pl.program_id(0)
    extent = image.shape[-1]
    turn = info[particle, 0]
    shift_x = info[particle, 1]
    shift_y = info[particle, 2]
    flip_x = turn >= 2
    flip_y = (turn == 1) | (turn == 2)
    move_x = jnp.where(flip_x, 1 - shift_x, shift_x) + SHIFT
    move_y = jnp.where(flip_y, 1 - shift_y, shift_y) + SHIFT
    odd = turn % 2 == 1

    @pl.when(odd)
    def _():
        turned[...] = image[0].T

    @pl.when(jnp.logical_not(odd))
    def _():
        turned[...] = image[0]

    along_x = jnp.dot(turned[...], columns[move_x], preferred_element_type=jnp.float32)
    spectrum = jnp.dot(
        rows[move_y], along_x.astype(jnp.bfloat16), preferred_element_type=jnp.float32
    )
    scale = defocus[info[particle, 3]] * (1.0 / (2.0 * math.pi))
    contrast = -sine_of_turns(radius[...] * scale + OFFSET_TURNS)
    half = extent // 2
    row_sine = lax.broadcasted_iota(jnp.int32, (extent, 1), 0) > half
    column_sine = lax.broadcasted_iota(jnp.int32, (1, extent), 1) > half
    sign_y = jnp.where(flip_y, -1.0, 1.0)
    sign_x = jnp.where(flip_x, -1.0, 1.0)
    signs = jnp.where(row_sine, sign_y, 1.0) * jnp.where(column_sine, sign_x, 1.0)
    weighted = (spectrum * (contrast * signs)).astype(jnp.bfloat16)
    low[0] = weighted[:, :half]
    high[0] = weighted[:, half:]


def class_kernel(sources, capacity, number, per_step, labels, block, slots, expand, *rest):
    outs, total = rest[:-1], rest[-1]
    step = pl.program_id(0)
    loads = sources

    @pl.when(step == 0)
    def _():
        total[...] = jnp.zeros_like(total)

    @pl.when(step < loads)
    def _():
        def body(particle, filled):
            label = labels[step * number + particle]
            mine = label // CLS_DEV == block[0]

            @pl.when(mine)
            def _():
                within = label % CLS_DEV
                total[within] += slots[filled].astype(jnp.float32)

            return filled + mine.astype(jnp.int32)

        lax.fori_loop(0, number, body, jnp.int32(0))

    @pl.when(step >= loads)
    def _():
        _, double, _ = outs[0].shape
        for item in range(per_step):
            value = total[(step - loads) * per_step + item].astype(jnp.bfloat16)
            laid = jnp.dot(expand[...], value, preferred_element_type=jnp.float32)
            laid = laid.astype(jnp.bfloat16)
            for part, out in enumerate(outs):
                out[item] = laid[part * double : (part + 1) * double]


def weight_kernel(labels, groups, block, defocus, radius, out):
    out[...] = jnp.zeros_like(out)

    def body(particle, carry):
        label = labels[particle]

        @pl.when(label // CLS_DEV == block[0])
        def _():
            scale = defocus[groups[particle]] * (1.0 / (2.0 * math.pi))
            contrast = sine_of_turns(radius[...] * scale + OFFSET_TURNS)
            within = label % CLS_DEV
            out[within] += contrast * contrast

        return carry

    lax.fori_loop(0, labels.shape[0], body, 0)


def final_kernel(per_step, parts, *refs):
    lows, highs, (weight, expand, out) = refs[:parts], refs[parts : 2 * parts], refs[2 * parts :]
    _, _, each, extent = out.shape
    for item in range(per_step):
        halves = []
        for received in (lows, highs):
            value = received[0][item].astype(jnp.float32)
            for part in received[1:]:
                value = value + part[item].astype(jnp.float32)
            halves.append(value.astype(jnp.bfloat16))
        value = jnp.concatenate(halves, axis=1)
        wide = jnp.dot(value, expand[...], preferred_element_type=jnp.float32)
        inverse = 1.0 / (weight[item] + WIENER_TERM)
        out[item, 0] = (wide[:each, :extent] + wide[each:, extent:]) * inverse
        out[item, 1] = (wide[:each, extent:] - wide[each:, :extent]) * inverse


def params():
    return pltpu.CompilerParams(vmem_limit_bytes=VMEM)


def per_device(images, class_block, class_within, rotation, shift, group, defocus):
    blocks = lax.axis_size("cls")
    parts = lax.axis_size("ptl")
    number, extent, _ = images.shape
    each = extent // parts
    capacity = 2 * number // blocks
    me = lax.axis_index("cls").astype(jnp.int32)
    part = lax.axis_index("ptl").astype(jnp.int32)
    target = class_block[:, 0]
    same = target[:, None] == target[None, :]
    before = jnp.arange(number)[:, None] > jnp.arange(number)[None, :]
    slot = target * capacity + jnp.sum((same & before).astype(jnp.int32), axis=1)
    info = jnp.stack([rotation, shift[:, 0], shift[:, 1], group], axis=1)

    klass = target * CLS_DEV + class_within
    own = jnp.stack([klass, group], axis=0)
    column = lax.all_to_all(
        jnp.broadcast_to(own[None], (blocks, 2, number)), "cls", 0, 0, tiled=True
    )
    frequency, _ = packed(extent)
    share = (frequency / extent) ** 2
    packed_radius = (share[:, None] + share[None, :]).astype(np.float32)
    row_table, column_table = tables(extent)

    whole = lambda shape: pl.BlockSpec(shape, lambda *_: (0,) * len(shape))
    half = extent // 2
    low, high = pl.pallas_call(
        transform_kernel,
        grid_spec=pltpu.PrefetchScalarGridSpec(
            num_scalar_prefetch=3,
            grid=(number,),
            in_specs=[
                pl.BlockSpec((1, extent, extent), lambda i, *_: (i, 0, 0)),
                whole(row_table.shape),
                whole(column_table.shape),
                whole((extent, extent)),
            ],
            out_specs=[pl.BlockSpec((1, extent, half), lambda i, slot, *_: (slot[i], 0, 0))] * 2,
            scratch_shapes=[pltpu.VMEM((extent, extent), jnp.bfloat16)],
        ),
        out_shape=[jax.ShapeDtypeStruct((blocks * capacity, extent, half), jnp.bfloat16)] * 2,
        compiler_params=params(),
        name="transform",
    )(slot, info, defocus, images, row_table, column_table, packed_radius)

    def to_class(outgoing):
        return lax.all_to_all(
            outgoing.reshape(blocks, capacity, extent, half), "cls", 0, 0, tiled=True
        ).reshape(blocks * capacity, extent, half)

    low, column = lax.optimization_barrier((low, column))
    labels = lax.all_to_all(
        jnp.broadcast_to(column[None], (parts, blocks, 2, number)), "ptl", 0, 0, tiled=True
    )
    all_class = labels[:, :, 0].reshape(-1)
    all_group = labels[:, :, 1].reshape(-1)
    column_class = column[:, 0].reshape(-1)
    low = to_class(low)
    low, high, all_class, all_group = lax.optimization_barrier((low, high, all_class, all_group))
    high = to_class(high)

    ky = part * each + jnp.arange(each, dtype=jnp.int32)
    kx = np.minimum(np.arange(extent), extent - np.arange(extent))
    ky = jnp.minimum(ky, extent - ky).astype(jnp.float32) / extent
    radius = ky[:, None] * ky[:, None] + ((kx / extent) ** 2).astype(np.float32)[None, :]
    smem = pl.BlockSpec(memory_space=pltpu.SMEM)
    vmem = pl.BlockSpec(memory_space=pltpu.VMEM)
    weight = pl.pallas_call(
        weight_kernel,
        in_specs=[smem, smem, smem, smem, vmem],
        out_specs=vmem,
        out_shape=jax.ShapeDtypeStruct((CLS_DEV, each, extent), jnp.float32),
        compiler_params=params(),
        cost_estimate=pl.CostEstimate(
            flops=40 * number * parts * each * extent, bytes_accessed=2**21, transcendentals=0
        ),
        name="weights",
    )(all_class, all_group, me[None], defocus, radius)

    per_step = 5
    steps = CLS_DEV // per_step
    expansion = jnp.roll(
        jnp.asarray(row_expansion(extent, parts)).reshape(parts, 2 * each, extent), -part, axis=0
    ).reshape(2 * extent, extent)

    def class_sums(arrived):
        sums = pl.pallas_call(
            functools.partial(class_kernel, blocks, capacity, number, per_step),
            grid_spec=pltpu.PrefetchScalarGridSpec(
                num_scalar_prefetch=2,
                grid=(blocks + steps,),
                in_specs=[
                    pl.BlockSpec(
                        (capacity, extent, half), lambda i, *_: (jnp.minimum(i, blocks - 1), 0, 0)
                    ),
                    whole((2 * extent, extent)),
                ],
                out_specs=[
                    pl.BlockSpec(
                        (per_step, 2 * each, half), lambda i, *_: (jnp.maximum(i - blocks, 0), 0, 0)
                    )
                ]
                * parts,
                scratch_shapes=[pltpu.VMEM((CLS_DEV, extent, half), jnp.float32)],
            ),
            out_shape=[jax.ShapeDtypeStruct((CLS_DEV, 2 * each, half), jnp.bfloat16)] * parts,
            compiler_params=params(),
            cost_estimate=pl.CostEstimate(
                flops=2 * CLS_DEV * 2 * extent * extent * half,
                bytes_accessed=2**23,
                transcendentals=0,
            ),
            name="classes",
        )(column_class, me[None], arrived, expansion)
        return [sums[0]] + [
            lax.ppermute(sums[by], "ptl", [(q, (q + by) % parts) for q in range(parts)])
            for by in range(1, parts)
        ]

    lows = class_sums(low)
    highs = class_sums(high)

    return pl.pallas_call(
        functools.partial(final_kernel, per_step, parts),
        grid=(steps,),
        in_specs=[pl.BlockSpec((per_step, 2 * each, half), lambda i: (i, 0, 0))] * (2 * parts)
        + [
            pl.BlockSpec((per_step, each, extent), lambda i: (i, 0, 0)),
            whole((extent, 2 * extent)),
        ],
        out_specs=pl.BlockSpec((per_step, 2, each, extent), lambda i: (i, 0, 0, 0)),
        out_shape=jax.ShapeDtypeStruct((CLS_DEV, 2, each, extent), jnp.float32),
        compiler_params=params(),
        name="finish",
    )(*lows, *highs, weight, column_expansion(extent))


def solution(mesh):
    return jax.shard_map(
        per_device,
        mesh=mesh,
        in_specs=(
            P(("cls", "ptl"), None, None),
            P(("cls", "ptl"), None),
            P(("cls", "ptl")),
            P(("cls", "ptl")),
            P(("cls", "ptl"), None),
            P(("cls", "ptl")),
            P(),
        ),
        out_specs=P("cls", None, "ptl", None),
        check_vma=False,
    )
```

```python
import functools
import math

import jax
import jax.numpy as jnp
import ml_dtypes
import numpy as np
from jax import lax
from jax.experimental import pallas as pl
from jax.experimental.pallas import tpu as pltpu
from jax.sharding import PartitionSpec as P

CLS_DEV = 25
SHIFT = 8
PHASE_CONTRAST = math.sqrt(0.99)
AMPLITUDE_CONTRAST = 0.1
WIENER_TERM = 1.0
OFFSET_TURNS = math.atan2(AMPLITUDE_CONTRAST, PHASE_CONTRAST) / (2.0 * math.pi)
VMEM = 48 * 1024 * 1024


def sine_coefficients():
    t = np.cos(np.linspace(0.0, math.pi / 2, 2001)[:-1]) / 2
    basis = np.stack([t ** (2 * i + 1) for i in range(7)], axis=1)
    return [float(c) for c in np.linalg.lstsq(basis, np.sin(2 * np.pi * t), rcond=None)[0]]


SINE = sine_coefficients()


def sine_of_turns(turns):
    t = turns - jnp.round(turns)
    square = t * t
    value = jnp.full_like(t, SINE[-1])
    for coefficient in SINE[-2::-1]:
        value = value * square + coefficient
    return value * t


def packed(extent):
    half = extent // 2
    index = np.arange(extent)
    is_sine = index > half
    return np.where(is_sine, index - half, index), is_sine


def tables(extent):
    frequency, is_sine = packed(extent)
    moves = np.arange(-SHIFT, SHIFT + 2)
    angle = frequency[None, :, None] * (np.arange(extent)[None, None, :] + moves[:, None, None])
    angle = (angle % extent) * (2.0 * math.pi / extent)
    value = np.where(is_sine[None, :, None], np.sin(angle), np.cos(angle)) / math.sqrt(extent)
    rows = value.astype(ml_dtypes.bfloat16)
    return rows, np.ascontiguousarray(rows.transpose(0, 2, 1))


def row_expansion(extent, parts):
    half = extent // 2
    each = extent // parts
    out = np.zeros((parts, 2, each, extent), np.float32)
    for ky in range(extent):
        size = min(ky, extent - ky)
        out[ky // each, 0, ky % each, size] = 1.0
        if 0 < size < half:
            out[ky // each, 1, ky % each, half + size] = 1.0 if ky < half else -1.0
    return out.reshape(2 * extent, extent).astype(ml_dtypes.bfloat16)


def column_expansion(extent):
    half = extent // 2
    out = np.zeros((extent, 2, extent), np.float32)
    for kx in range(extent):
        size = min(kx, extent - kx)
        out[size, 0, kx] = 1.0
        if 0 < size < half:
            out[half + size, 1, kx] = -1.0 if kx < half else 1.0
    return out.reshape(extent, 2 * extent).astype(ml_dtypes.bfloat16)


def transform_kernel(slot, info, defocus, image, rows, columns, radius, low, high, turned):
    particle = pl.program_id(0)
    extent = image.shape[-1]
    turn = info[particle, 0]
    shift_x = info[particle, 1]
    shift_y = info[particle, 2]
    flip_x = turn >= 2
    flip_y = (turn == 1) | (turn == 2)
    move_x = jnp.where(flip_x, 1 - shift_x, shift_x) + SHIFT
    move_y = jnp.where(flip_y, 1 - shift_y, shift_y) + SHIFT
    odd = turn % 2 == 1

    @pl.when(odd)
    def _():
        turned[...] = image[0].T

    @pl.when(jnp.logical_not(odd))
    def _():
        turned[...] = image[0]

    along_x = jnp.dot(turned[...], columns[move_x], preferred_element_type=jnp.float32)
    spectrum = jnp.dot(
        rows[move_y], along_x.astype(jnp.bfloat16), preferred_element_type=jnp.float32
    )
    scale = defocus[info[particle, 3]] * (1.0 / (2.0 * math.pi))
    contrast = -sine_of_turns(radius[...] * scale + OFFSET_TURNS)
    half = extent // 2
    row_sine = lax.broadcasted_iota(jnp.int32, (extent, 1), 0) > half
    column_sine = lax.broadcasted_iota(jnp.int32, (1, extent), 1) > half
    sign_y = jnp.where(flip_y, -1.0, 1.0)
    sign_x = jnp.where(flip_x, -1.0, 1.0)
    signs = jnp.where(row_sine, sign_y, 1.0) * jnp.where(column_sine, sign_x, 1.0)
    weighted = (spectrum * (contrast * signs)).astype(jnp.bfloat16)
    low[0] = weighted[:, :half]
    high[0] = weighted[:, half:]


def class_kernel(sources, capacity, number, per_step, labels, block, slots, expand, *rest):
    outs, total = rest[:-1], rest[-1]
    step = pl.program_id(0)
    loads = sources

    @pl.when(step == 0)
    def _():
        total[...] = jnp.zeros_like(total)

    @pl.when(step < loads)
    def _():
        def body(particle, filled):
            label = labels[step * number + particle]
            mine = label // CLS_DEV == block[0]

            @pl.when(mine)
            def _():
                within = label % CLS_DEV
                total[within] += slots[filled].astype(jnp.float32)

            return filled + mine.astype(jnp.int32)

        lax.fori_loop(0, number, body, jnp.int32(0))

    @pl.when(step >= loads)
    def _():
        _, double, _ = outs[0].shape
        for item in range(per_step):
            value = total[(step - loads) * per_step + item].astype(jnp.bfloat16)
            laid = jnp.dot(expand[...], value, preferred_element_type=jnp.float32)
            laid = laid.astype(jnp.bfloat16)
            for part, out in enumerate(outs):
                out[item] = laid[part * double : (part + 1) * double]


def weight_kernel(labels, groups, block, defocus, radius, out):
    out[...] = jnp.zeros_like(out)

    def body(particle, carry):
        label = labels[particle]

        @pl.when(label // CLS_DEV == block[0])
        def _():
            scale = defocus[groups[particle]] * (1.0 / (2.0 * math.pi))
            contrast = sine_of_turns(radius[...] * scale + OFFSET_TURNS)
            within = label % CLS_DEV
            out[within] += contrast * contrast

        return carry

    lax.fori_loop(0, labels.shape[0], body, 0)


def final_kernel(per_step, parts, *refs):
    lows, highs, (weight, expand, out) = refs[:parts], refs[parts : 2 * parts], refs[2 * parts :]
    _, _, each, extent = out.shape
    for item in range(per_step):
        halves = []
        for received in (lows, highs):
            value = received[0][item].astype(jnp.float32)
            for part in received[1:]:
                value = value + part[item].astype(jnp.float32)
            halves.append(value.astype(jnp.bfloat16))
        value = jnp.concatenate(halves, axis=1)
        wide = jnp.dot(value, expand[...], preferred_element_type=jnp.float32)
        inverse = 1.0 / (weight[item] + WIENER_TERM)
        out[item, 0] = (wide[:each, :extent] + wide[each:, extent:]) * inverse
        out[item, 1] = (wide[:each, extent:] - wide[each:, :extent]) * inverse


def params():
    return pltpu.CompilerParams(vmem_limit_bytes=VMEM)


def per_device(images, class_block, class_within, rotation, shift, group, defocus):
    blocks = lax.axis_size("cls")
    parts = lax.axis_size("ptl")
    number, extent, _ = images.shape
    each = extent // parts
    capacity = 2 * number // blocks
    me = lax.axis_index("cls").astype(jnp.int32)
    part = lax.axis_index("ptl").astype(jnp.int32)
    target = class_block[:, 0]
    same = target[:, None] == target[None, :]
    before = jnp.arange(number)[:, None] > jnp.arange(number)[None, :]
    slot = target * capacity + jnp.sum((same & before).astype(jnp.int32), axis=1)
    info = jnp.stack([rotation, shift[:, 0], shift[:, 1], group], axis=1)

    klass = target * CLS_DEV + class_within
    own = jnp.stack([klass, group], axis=0)
    column = lax.all_to_all(
        jnp.broadcast_to(own[None], (blocks, 2, number)), "cls", 0, 0, tiled=True
    )
    frequency, _ = packed(extent)
    share = (frequency / extent) ** 2
    packed_radius = (share[:, None] + share[None, :]).astype(np.float32)
    row_table, column_table = tables(extent)

    whole = lambda shape: pl.BlockSpec(shape, lambda *_: (0,) * len(shape))
    half = extent // 2
    low, high = pl.pallas_call(
        transform_kernel,
        grid_spec=pltpu.PrefetchScalarGridSpec(
            num_scalar_prefetch=3,
            grid=(number,),
            in_specs=[
                pl.BlockSpec((1, extent, extent), lambda i, *_: (i, 0, 0)),
                whole(row_table.shape),
                whole(column_table.shape),
                whole((extent, extent)),
            ],
            out_specs=[pl.BlockSpec((1, extent, half), lambda i, slot, *_: (slot[i], 0, 0))] * 2,
            scratch_shapes=[pltpu.VMEM((extent, extent), jnp.bfloat16)],
        ),
        out_shape=[jax.ShapeDtypeStruct((blocks * capacity, extent, half), jnp.bfloat16)] * 2,
        compiler_params=params(),
        name="transform",
    )(slot, info, defocus, images, row_table, column_table, packed_radius)

    def to_class(outgoing):
        return lax.all_to_all(
            outgoing.reshape(blocks, capacity, extent, half), "cls", 0, 0, tiled=True
        ).reshape(blocks * capacity, extent, half)

    low, column = lax.optimization_barrier((low, column))
    labels = jnp.stack(
        [column]
        + [
            lax.ppermute(column, "ptl", [(q, (q + by) % parts) for q in range(parts)])
            for by in range(1, parts)
        ]
    )
    all_class = labels[:, :, 0].reshape(-1)
    all_group = labels[:, :, 1].reshape(-1)
    column_class = column[:, 0].reshape(-1)
    low = to_class(low)
    low, high = lax.optimization_barrier((low, high))
    high = to_class(high)

    ky = part * each + jnp.arange(each, dtype=jnp.int32)
    kx = np.minimum(np.arange(extent), extent - np.arange(extent))
    ky = jnp.minimum(ky, extent - ky).astype(jnp.float32) / extent
    radius = ky[:, None] * ky[:, None] + ((kx / extent) ** 2).astype(np.float32)[None, :]
    smem = pl.BlockSpec(memory_space=pltpu.SMEM)
    vmem = pl.BlockSpec(memory_space=pltpu.VMEM)
    weight = pl.pallas_call(
        weight_kernel,
        in_specs=[smem, smem, smem, smem, vmem],
        out_specs=vmem,
        out_shape=jax.ShapeDtypeStruct((CLS_DEV, each, extent), jnp.float32),
        compiler_params=params(),
        cost_estimate=pl.CostEstimate(
            flops=40 * number * parts * each * extent, bytes_accessed=2**21, transcendentals=0
        ),
        name="weights",
    )(all_class, all_group, me[None], defocus, radius)

    per_step = 5
    steps = CLS_DEV // per_step
    expansion = jnp.roll(
        jnp.asarray(row_expansion(extent, parts)).reshape(parts, 2 * each, extent), -part, axis=0
    ).reshape(2 * extent, extent)

    def class_sums(arrived):
        sums = pl.pallas_call(
            functools.partial(class_kernel, blocks, capacity, number, per_step),
            grid_spec=pltpu.PrefetchScalarGridSpec(
                num_scalar_prefetch=2,
                grid=(blocks + steps,),
                in_specs=[
                    pl.BlockSpec(
                        (capacity, extent, half), lambda i, *_: (jnp.minimum(i, blocks - 1), 0, 0)
                    ),
                    whole((2 * extent, extent)),
                ],
                out_specs=[
                    pl.BlockSpec(
                        (per_step, 2 * each, half), lambda i, *_: (jnp.maximum(i - blocks, 0), 0, 0)
                    )
                ]
                * parts,
                scratch_shapes=[pltpu.VMEM((CLS_DEV, extent, half), jnp.float32)],
            ),
            out_shape=[jax.ShapeDtypeStruct((CLS_DEV, 2 * each, half), jnp.bfloat16)] * parts,
            compiler_params=params(),
            cost_estimate=pl.CostEstimate(
                flops=2 * CLS_DEV * 2 * extent * extent * half,
                bytes_accessed=2**23,
                transcendentals=0,
            ),
            name="classes",
        )(column_class, me[None], arrived, expansion)
        return [sums[0]] + [
            lax.ppermute(sums[by], "ptl", [(q, (q + by) % parts) for q in range(parts)])
            for by in range(1, parts)
        ]

    lows = class_sums(low)
    highs = class_sums(high)

    return pl.pallas_call(
        functools.partial(final_kernel, per_step, parts),
        grid=(steps,),
        in_specs=[pl.BlockSpec((per_step, 2 * each, half), lambda i: (i, 0, 0))] * (2 * parts)
        + [
            pl.BlockSpec((per_step, each, extent), lambda i: (i, 0, 0)),
            whole((extent, 2 * extent)),
        ],
        out_specs=pl.BlockSpec((per_step, 2, each, extent), lambda i: (i, 0, 0, 0)),
        out_shape=jax.ShapeDtypeStruct((CLS_DEV, 2, each, extent), jnp.float32),
        compiler_params=params(),
        name="finish",
    )(*lows, *highs, weight, column_expansion(extent))


def solution(mesh):
    return jax.shard_map(
        per_device,
        mesh=mesh,
        in_specs=(
            P(("cls", "ptl"), None, None),
            P(("cls", "ptl"), None),
            P(("cls", "ptl")),
            P(("cls", "ptl")),
            P(("cls", "ptl"), None),
            P(("cls", "ptl")),
            P(),
        ),
        out_specs=P("cls", None, "ptl", None),
        check_vma=False,
    )
```

```python
import functools
import math

import jax
import jax.numpy as jnp
import ml_dtypes
import numpy as np
from jax import lax
from jax.experimental import pallas as pl
from jax.experimental.pallas import tpu as pltpu
from jax.sharding import PartitionSpec as P

CLS_DEV = 25
SHIFT = 8
PHASE_CONTRAST = math.sqrt(0.99)
AMPLITUDE_CONTRAST = 0.1
WIENER_TERM = 1.0
OFFSET_TURNS = math.atan2(AMPLITUDE_CONTRAST, PHASE_CONTRAST) / (2.0 * math.pi)
VMEM = 48 * 1024 * 1024


def sine_coefficients():
    t = np.cos(np.linspace(0.0, math.pi / 2, 2001)[:-1]) / 2
    basis = np.stack([t ** (2 * i + 1) for i in range(7)], axis=1)
    return [float(c) for c in np.linalg.lstsq(basis, np.sin(2 * np.pi * t), rcond=None)[0]]


SINE = sine_coefficients()


def sine_of_turns(turns):
    t = turns - jnp.round(turns)
    square = t * t
    value = jnp.full_like(t, SINE[-1])
    for coefficient in SINE[-2::-1]:
        value = value * square + coefficient
    return value * t


def packed(extent):
    half = extent // 2
    index = np.arange(extent)
    is_sine = index > half
    return np.where(is_sine, index - half, index), is_sine


def tables(extent):
    frequency, is_sine = packed(extent)
    moves = np.arange(-SHIFT, SHIFT + 2)
    angle = frequency[None, :, None] * (np.arange(extent)[None, None, :] + moves[:, None, None])
    angle = (angle % extent) * (2.0 * math.pi / extent)
    value = np.where(is_sine[None, :, None], np.sin(angle), np.cos(angle)) / math.sqrt(extent)
    rows = value.astype(ml_dtypes.bfloat16)
    return rows, np.ascontiguousarray(rows.transpose(0, 2, 1))


def row_expansion(extent, parts):
    half = extent // 2
    each = extent // parts
    out = np.zeros((parts, 2, each, extent), np.float32)
    for ky in range(extent):
        size = min(ky, extent - ky)
        out[ky // each, 0, ky % each, size] = 1.0
        if 0 < size < half:
            out[ky // each, 1, ky % each, half + size] = 1.0 if ky < half else -1.0
    return out.reshape(2 * extent, extent).astype(ml_dtypes.bfloat16)


def column_expansion(extent):
    half = extent // 2
    out = np.zeros((extent, 2, extent), np.float32)
    for kx in range(extent):
        size = min(kx, extent - kx)
        out[size, 0, kx] = 1.0
        if 0 < size < half:
            out[half + size, 1, kx] = -1.0 if kx < half else 1.0
    return out.reshape(extent, 2 * extent).astype(ml_dtypes.bfloat16)


def transform_kernel(slot, info, defocus, image, rows, columns, radius, low, high, turned):
    particle = pl.program_id(0)
    extent = image.shape[-1]
    turn = info[particle, 0]
    shift_x = info[particle, 1]
    shift_y = info[particle, 2]
    flip_x = turn >= 2
    flip_y = (turn == 1) | (turn == 2)
    move_x = jnp.where(flip_x, 1 - shift_x, shift_x) + SHIFT
    move_y = jnp.where(flip_y, 1 - shift_y, shift_y) + SHIFT
    odd = turn % 2 == 1

    @pl.when(odd)
    def _():
        turned[...] = image[0].T

    @pl.when(jnp.logical_not(odd))
    def _():
        turned[...] = image[0]

    along_x = jnp.dot(turned[...], columns[move_x], preferred_element_type=jnp.float32)
    spectrum = jnp.dot(
        rows[move_y], along_x.astype(jnp.bfloat16), preferred_element_type=jnp.float32
    )
    scale = defocus[info[particle, 3]] * (1.0 / (2.0 * math.pi))
    contrast = -sine_of_turns(radius[...] * scale + OFFSET_TURNS)
    half = extent // 2
    row_sine = lax.broadcasted_iota(jnp.int32, (extent, 1), 0) > half
    column_sine = lax.broadcasted_iota(jnp.int32, (1, extent), 1) > half
    sign_y = jnp.where(flip_y, -1.0, 1.0)
    sign_x = jnp.where(flip_x, -1.0, 1.0)
    signs = jnp.where(row_sine, sign_y, 1.0) * jnp.where(column_sine, sign_x, 1.0)
    weighted = (spectrum * (contrast * signs)).astype(jnp.bfloat16)
    low[0] = weighted[:, :half]
    high[0] = weighted[:, half:]


def class_kernel(sources, capacity, number, per_step, labels, block, slots, expand, *rest):
    outs, total = rest[:-1], rest[-1]
    step = pl.program_id(0)
    loads = sources

    @pl.when(step == 0)
    def _():
        total[...] = jnp.zeros_like(total)

    @pl.when(step < loads)
    def _():
        def body(particle, filled):
            label = labels[step * number + particle]
            mine = label // CLS_DEV == block[0]

            @pl.when(mine)
            def _():
                within = label % CLS_DEV
                total[within] += slots[filled].astype(jnp.float32)

            return filled + mine.astype(jnp.int32)

        lax.fori_loop(0, number, body, jnp.int32(0))

    @pl.when(step >= loads)
    def _():
        _, double, _ = outs[0].shape
        for item in range(per_step):
            value = total[(step - loads) * per_step + item].astype(jnp.bfloat16)
            laid = jnp.dot(expand[...], value, preferred_element_type=jnp.float32)
            laid = laid.astype(jnp.bfloat16)
            for part, out in enumerate(outs):
                out[item] = laid[part * double : (part + 1) * double]


def weight_kernel(labels, groups, block, defocus, radius, out):
    out[...] = jnp.zeros_like(out)

    def body(particle, carry):
        label = labels[particle]

        @pl.when(label // CLS_DEV == block[0])
        def _():
            scale = defocus[groups[particle]] * (1.0 / (2.0 * math.pi))
            contrast = sine_of_turns(radius[...] * scale + OFFSET_TURNS)
            within = label % CLS_DEV
            out[within] += contrast * contrast

        return carry

    lax.fori_loop(0, labels.shape[0], body, 0)


def final_kernel(per_step, parts, *refs):
    lows, highs, (weight, expand, out) = refs[:parts], refs[parts : 2 * parts], refs[2 * parts :]
    _, _, each, extent = out.shape
    for item in range(per_step):
        halves = []
        for received in (lows, highs):
            value = received[0][item].astype(jnp.float32)
            for part in received[1:]:
                value = value + part[item].astype(jnp.float32)
            halves.append(value.astype(jnp.bfloat16))
        value = jnp.concatenate(halves, axis=1)
        wide = jnp.dot(value, expand[...], preferred_element_type=jnp.float32)
        inverse = 1.0 / (weight[item] + WIENER_TERM)
        out[item, 0] = (wide[:each, :extent] + wide[each:, extent:]) * inverse
        out[item, 1] = (wide[:each, extent:] - wide[each:, :extent]) * inverse


def params():
    return pltpu.CompilerParams(vmem_limit_bytes=VMEM)


def per_device(images, class_block, class_within, rotation, shift, group, defocus):
    blocks = lax.axis_size("cls")
    parts = lax.axis_size("ptl")
    number, extent, _ = images.shape
    each = extent // parts
    capacity = 2 * number // blocks
    me = lax.axis_index("cls").astype(jnp.int32)
    part = lax.axis_index("ptl").astype(jnp.int32)
    target = class_block[:, 0]
    same = target[:, None] == target[None, :]
    before = jnp.arange(number)[:, None] > jnp.arange(number)[None, :]
    slot = target * capacity + jnp.sum((same & before).astype(jnp.int32), axis=1)
    info = jnp.stack([rotation, shift[:, 0], shift[:, 1], group], axis=1)

    klass = target * CLS_DEV + class_within
    own = jnp.stack([klass, group], axis=0)
    column = lax.all_to_all(
        jnp.broadcast_to(own[None], (blocks, 2, number)), "cls", 0, 0, tiled=True
    )
    frequency, _ = packed(extent)
    share = (frequency / extent) ** 2
    packed_radius = (share[:, None] + share[None, :]).astype(np.float32)
    row_table, column_table = tables(extent)

    whole = lambda shape: pl.BlockSpec(shape, lambda *_: (0,) * len(shape))
    half = extent // 2
    low, high = pl.pallas_call(
        transform_kernel,
        grid_spec=pltpu.PrefetchScalarGridSpec(
            num_scalar_prefetch=3,
            grid=(number,),
            in_specs=[
                pl.BlockSpec((1, extent, extent), lambda i, *_: (i, 0, 0)),
                whole(row_table.shape),
                whole(column_table.shape),
                whole((extent, extent)),
            ],
            out_specs=[pl.BlockSpec((1, extent, half), lambda i, slot, *_: (slot[i], 0, 0))] * 2,
            scratch_shapes=[pltpu.VMEM((extent, extent), jnp.bfloat16)],
        ),
        out_shape=[jax.ShapeDtypeStruct((blocks * capacity, extent, half), jnp.bfloat16)] * 2,
        compiler_params=params(),
        name="transform",
    )(slot, info, defocus, images, row_table, column_table, packed_radius)

    def to_class(outgoing):
        return lax.all_to_all(
            outgoing.reshape(blocks, capacity, extent, half), "cls", 0, 0, tiled=True
        ).reshape(blocks * capacity, extent, half)

    low, column = lax.optimization_barrier((low, column))
    labels = jnp.stack(
        [column]
        + [
            lax.ppermute(column, "ptl", [(q, (q + by) % parts) for q in range(parts)])
            for by in range(1, parts)
        ]
    )
    all_class = labels[:, :, 0].reshape(-1)
    all_group = labels[:, :, 1].reshape(-1)
    column_class = column[:, 0].reshape(-1)
    low = to_class(low)
    low, high, all_class, all_group = lax.optimization_barrier((low, high, all_class, all_group))
    high = to_class(high)

    ky = part * each + jnp.arange(each, dtype=jnp.int32)
    kx = np.minimum(np.arange(extent), extent - np.arange(extent))
    ky = jnp.minimum(ky, extent - ky).astype(jnp.float32) / extent
    radius = ky[:, None] * ky[:, None] + ((kx / extent) ** 2).astype(np.float32)[None, :]
    smem = pl.BlockSpec(memory_space=pltpu.SMEM)
    vmem = pl.BlockSpec(memory_space=pltpu.VMEM)
    weight = pl.pallas_call(
        weight_kernel,
        in_specs=[smem, smem, smem, smem, vmem],
        out_specs=vmem,
        out_shape=jax.ShapeDtypeStruct((CLS_DEV, each, extent), jnp.float32),
        compiler_params=params(),
        cost_estimate=pl.CostEstimate(
            flops=40 * number * parts * each * extent, bytes_accessed=2**21, transcendentals=0
        ),
        name="weights",
    )(all_class, all_group, me[None], defocus, radius)

    per_step = 5
    steps = CLS_DEV // per_step
    expansion = jnp.roll(
        jnp.asarray(row_expansion(extent, parts)).reshape(parts, 2 * each, extent), -part, axis=0
    ).reshape(2 * extent, extent)

    def class_sums(arrived):
        sums = pl.pallas_call(
            functools.partial(class_kernel, blocks, capacity, number, per_step),
            grid_spec=pltpu.PrefetchScalarGridSpec(
                num_scalar_prefetch=2,
                grid=(blocks + steps,),
                in_specs=[
                    pl.BlockSpec(
                        (capacity, extent, half), lambda i, *_: (jnp.minimum(i, blocks - 1), 0, 0)
                    ),
                    whole((2 * extent, extent)),
                ],
                out_specs=[
                    pl.BlockSpec(
                        (per_step, 2 * each, half), lambda i, *_: (jnp.maximum(i - blocks, 0), 0, 0)
                    )
                ]
                * parts,
                scratch_shapes=[pltpu.VMEM((CLS_DEV, extent, half), jnp.float32)],
            ),
            out_shape=[jax.ShapeDtypeStruct((CLS_DEV, 2 * each, half), jnp.bfloat16)] * parts,
            compiler_params=params(),
            cost_estimate=pl.CostEstimate(
                flops=2 * CLS_DEV * 2 * extent * extent * half,
                bytes_accessed=2**23,
                transcendentals=0,
            ),
            name="classes",
        )(column_class, me[None], arrived, expansion)
        return [sums[0]] + [
            lax.ppermute(sums[by], "ptl", [(q, (q + by) % parts) for q in range(parts)])
            for by in range(1, parts)
        ]

    lows = class_sums(low)
    highs = class_sums(high)

    return pl.pallas_call(
        functools.partial(final_kernel, per_step, parts),
        grid=(steps,),
        in_specs=[pl.BlockSpec((per_step, 2 * each, half), lambda i: (i, 0, 0))] * (2 * parts)
        + [
            pl.BlockSpec((per_step, each, extent), lambda i: (i, 0, 0)),
            whole((extent, 2 * extent)),
        ],
        out_specs=pl.BlockSpec((per_step, 2, each, extent), lambda i: (i, 0, 0, 0)),
        out_shape=jax.ShapeDtypeStruct((CLS_DEV, 2, each, extent), jnp.float32),
        compiler_params=params(),
        name="finish",
    )(*lows, *highs, weight, column_expansion(extent))


def solution(mesh):
    return jax.shard_map(
        per_device,
        mesh=mesh,
        in_specs=(
            P(("cls", "ptl"), None, None),
            P(("cls", "ptl"), None),
            P(("cls", "ptl")),
            P(("cls", "ptl")),
            P(("cls", "ptl"), None),
            P(("cls", "ptl")),
            P(),
        ),
        out_specs=P("cls", None, "ptl", None),
        check_vma=False,
    )
```
